32 devices in a mesh: cuts: 8 (over z, y), angle: 4 (over x, core).
Axes of the slice: x: 2, y: 2, z: 4, core: 2. Of those that a mesh axis runs over, the one named last changes fastest.
Arguments:
- density: bfloat16 [8, 576, 256], P('cuts', 'angle'), may hold values from 0.049804688 to 2
- kernel_blocks: bfloat16 [576, 256, 384], P('cuts'), may hold values from -0.015625 to 0.015625
Outputs:
- sinogram: bfloat16 [8, 576, 384], P('cuts', 'angle')
The draws below stay inside these ranges and needn't reach their ends.
All inputs are finite; a program needn't handle non-finite values.
Results may differ from the reference program's by a relative error of at most 0.0012.
Values may be sent and summed in bfloat16 or wider, within the bound.
A program may use at most 128 MiB of HBM per device.

```python
import math
import jax
import jax.numpy as jnp

NA = 576
R = 256
B = 384
SLICES = 8


def block_scale(key, shape, shards, low, high):
    def one(axis_at, parts):
        draws = jax.random.uniform(jax.random.fold_in(jax.random.fold_in(key, 6), axis_at), (parts,), jnp.float32, low / len(shards), high / len(shards))
        return jnp.repeat(jnp.exp(draws), shape[axis_at] // parts).reshape((-1,) + (1,) * (len(shape) - axis_at - 1))

    factor_of = one(*shards[0])
    for cut in shards[1:]:
        factor_of = factor_of * one(*cut)
    return factor_of


def bell_draw(own_key, extent, spread, bound, cuts=(), dtype=jnp.bfloat16):
    array = jax.random.normal(own_key, extent, jnp.float32) * spread
    if len(cuts) > 0:
        array = block_scale(own_key, extent, cuts, -0.22, 0.18) * array
    return jnp.clip(array, min=-bound, max=bound).astype(dtype)


def setup_inputs(seed: int = 0) -> dict:
    seeds = jax.random.split(jax.random.key(seed), 3)
    density = jnp.clip(jnp.exp(math.log(2.0) - 3.6927934 * jax.random.uniform(seeds[0], (SLICES, NA, R), jnp.float32) ** block_scale(seeds[0], (SLICES, NA, R), ((0, 8), (1, 4)), -0.2, 0.2)), 0.049804688, 2.0).astype(jnp.bfloat16)
    kernel_blocks = bell_draw(seeds[1], (NA, R, B), (NA * R) ** -0.5, 0.015625, ((0, 8),))
    return {"density": density, "kernel_blocks": kernel_blocks}


def reference(density, kernel_blocks):
    spectrum_image = jnp.fft.rfft(density.astype(jnp.float32), axis=1)
    spectrum_kernel = jnp.fft.rfft(kernel_blocks.astype(jnp.float32), axis=0)
    product_freq = jnp.einsum("skr,krb->skb", spectrum_image, spectrum_kernel)
    contribution = jnp.fft.irfft(product_freq, n=NA, axis=1)
    return contribution.astype(jnp.bfloat16)
```

```python
import functools
import jax
import jax.numpy as jnp
from jax import lax
from jax.experimental import pallas as pl
from jax.experimental.pallas import tpu as pltpu
from jax.sharding import PartitionSpec as P

MESH = pl.DeviceIdType.MESH


def split_of(count, options):
    for n in options:
        if count % n == 0:
            return n
    return 1


def project_kernel(cuts, views, offsets, slices, group, chunk, w_ref, k_ref, out_ref,
                   k_buf, acc, tmp, part, y_recv, z_recv,
                   k_sem, ys_sem, yr_sem, zs_sem, zr_sem):
    bins = out_ref.shape[-1]
    slabs = bins // 128
    depth = cuts // 2
    steps = offsets // (2 * group)
    chunks = views // chunk
    rows = (chunk + 2) * slices
    cut = lax.axis_index("cuts")
    ang = lax.axis_index("angle")
    z, y = cut // 2, cut % 2
    first = views - (cut * offsets) % views - 2

    def k_copy(step):
        at = pl.ds(step * 2 * group, 2 * group)
        return pltpu.make_async_copy(k_ref.at[at], k_buf.at[at], k_sem.at[step])

    for step in range(steps):
        k_copy(step).start()

    barrier = pltpu.get_barrier_semaphore()
    pl.semaphore_signal(barrier, inc=1, device_id=(2 * z + 1 - y, ang), device_id_type=MESH)
    for d in range(1, depth):
        pl.semaphore_signal(barrier, inc=1, device_id=(2 * lax.rem(z + d, depth) + y, ang), device_id_type=MESH)
    pl.semaphore_wait(barrier, depth)

    def y_copy(m):
        return pltpu.make_async_remote_copy(
            src_ref=part.at[m, 1 - y], dst_ref=y_recv.at[m],
            send_sem=ys_sem.at[m], recv_sem=yr_sem.at[m],
            device_id=(2 * z + 1 - y, ang), device_id_type=MESH)

    def z_copy(m, d):
        peer = lax.rem(z + d, depth)
        return pltpu.make_async_remote_copy(
            src_ref=part.at[m, y, peer], dst_ref=z_recv.at[m, d - 1],
            send_sem=zs_sem.at[m, d - 1], recv_sem=zr_sem.at[m, d - 1],
            device_id=(2 * peer + y, ang), device_id_type=MESH)

    def z_stage(m):
        y_copy(m).wait_recv()
        part[m, y] += y_recv[m]
        for d in range(depth - 1, 0, -1):
            z_copy(m, d).start()

    for m in range(chunks):
        def body(step, _):
            if m == 0:
                k_copy(step).wait()
            left, right = [], []
            for n in range(group):
                pair = step * group + n
                row = pl.multiple_of((first - 2 * pair + m * chunk) * slices, 16)
                left.append(w_ref[pl.ds(row, rows), :])
                right.append(jnp.concatenate([k_buf[2 * pair], k_buf[2 * pair + 1]], axis=1))
            product = jnp.dot(jnp.concatenate(left, axis=1), jnp.concatenate(right, axis=0),
                              preferred_element_type=jnp.float32)

            @pl.when(step == 0)
            def _():
                acc[...] = product

            @pl.when(step > 0)
            def _():
                acc[...] += product

            return 0

        lax.fori_loop(0, steps, body, 0)
        for b in range(slabs):
            tmp[b] = (acc[slices:slices + chunk * slices, 128 * b:128 * (b + 1)]
                      + acc[:chunk * slices, bins + 128 * b:bins + 128 * (b + 1)])
        for s in range(slices):
            for b in range(slabs):
                part[m, s % 2, s // 2, :, 128 * b:128 * (b + 1)] = tmp[b, pl.ds(s, chunk, stride=slices), :]
        y_copy(m).start()
        if m > 0:
            z_stage(m - 1)
    z_stage(chunks - 1)
    for m in range(chunks):
        total = part[m, y, z]
        for d in range(1, depth):
            z_copy(m, d).wait_recv()
            total += z_recv[m, d - 1]
        out_ref[0, m * chunk:(m + 1) * chunk, :] = total.astype(out_ref.dtype)
    for m in range(chunks):
        y_copy(m).wait_send()
        for d in range(1, depth):
            z_copy(m, d).wait_send()


def project(window, kernel_blocks, cuts, views, slices):
    offsets, radii, bins = kernel_blocks.shape
    group = split_of(offsets // 2, (3, 2))
    chunk = 48 if views % 48 == 0 else views
    chunks, depth = views // chunk, cuts // 2
    rows = (chunk + 2) * slices
    return pl.pallas_call(
        functools.partial(project_kernel, cuts, views, offsets, slices, group, chunk),
        out_shape=jax.ShapeDtypeStruct((1, views, bins), jnp.bfloat16),
        in_specs=[pl.BlockSpec(memory_space=pltpu.VMEM), pl.BlockSpec(memory_space=pl.ANY)],
        out_specs=pl.BlockSpec(memory_space=pltpu.VMEM),
        scratch_shapes=[
            pltpu.VMEM((offsets, radii, bins), jnp.bfloat16),
            pltpu.VMEM((rows, 2 * bins), jnp.float32),
            pltpu.VMEM((bins // 128, chunk * slices, 128), jnp.float32),
            pltpu.VMEM((chunks, 2, depth, chunk, bins), jnp.float32),
            pltpu.VMEM((chunks, depth, chunk, bins), jnp.float32),
            pltpu.VMEM((chunks, depth - 1, chunk, bins), jnp.float32),
            pltpu.SemaphoreType.DMA((offsets // (2 * group),)),
            pltpu.SemaphoreType.DMA((chunks,)),
            pltpu.SemaphoreType.DMA((chunks,)),
            pltpu.SemaphoreType.DMA((chunks, depth - 1)),
            pltpu.SemaphoreType.DMA((chunks, depth - 1)),
        ],
        compiler_params=pltpu.CompilerParams(
            collective_id=0, has_side_effects=True, vmem_limit_bytes=44 * 2**20),
        cost_estimate=pl.CostEstimate(
            flops=2 * views * slices * offsets * radii * bins,
            bytes_accessed=2 * offsets * radii * bins, transcendentals=0),
        name="project",
    )(window, kernel_blocks)


def local(density, kernel_blocks):
    angles_dev = density.shape[1]
    offsets_dev = kernel_blocks.shape[0]
    angle_count = lax.axis_size("angle")
    cuts = lax.axis_size("cuts")
    offset_start = lax.axis_index("cuts") * offsets_dev
    block_steps = offset_start // angles_dev
    gathered = lax.all_gather(density, "cuts", axis=0, tiled=True)
    slices, _, radii = gathered.shape
    full_cycle = lax.all_gather(gathered, "angle", axis=1, tiled=True)
    doubled = jnp.concatenate([full_cycle, full_cycle[:, :angles_dev]], axis=1)
    window_start = (lax.axis_index("angle") - block_steps - 1) % angle_count * angles_dev
    window = lax.dynamic_slice_in_dim(doubled, window_start, 2 * angles_dev, 1)
    rows = jnp.roll(jnp.swapaxes(window, 0, 1), -1, axis=0).reshape(2 * angles_dev * slices, radii)
    return project(rows, kernel_blocks, cuts, angles_dev, slices)


def solution(mesh):
    return jax.shard_map(
        local,
        mesh=mesh,
        in_specs=(P("cuts", "angle", None), P("cuts", None, None)),
        out_specs=P("cuts", "angle", None),
        check_vma=False,
    )
```

```python
import functools
import jax
import jax.numpy as jnp
from jax import lax
from jax.experimental import pallas as pl
from jax.experimental.pallas import tpu as pltpu
from jax.sharding import PartitionSpec as P

MESH = pl.DeviceIdType.MESH


def split_of(count, options):
    for n in options:
        if count % n == 0:
            return n
    return 1


def project_kernel(cuts, views, offsets, slices, group, chunk, w_ref, k_ref, out_ref,
                   k_buf, acc, tmp, part, y_recv, z_recv,
                   k_sem, ys_sem, yr_sem, zs_sem, zr_sem):
    bins = out_ref.shape[-1]
    slabs = bins // 128
    depth = cuts // 2
    steps = offsets // (2 * group)
    chunks = views // chunk
    rows = (chunk + 2) * slices
    cut = lax.axis_index("cuts")
    ang = lax.axis_index("angle")
    z, y = cut // 2, cut % 2
    first = views - (cut * offsets) % views - 2

    def k_copy(step):
        at = pl.ds(step * 2 * group, 2 * group)
        return pltpu.make_async_copy(k_ref.at[at], k_buf.at[at], k_sem.at[step])

    for step in range(steps):
        k_copy(step).start()

    barrier = pltpu.get_barrier_semaphore()
    pl.semaphore_signal(barrier, inc=1, device_id=(2 * z + 1 - y, ang), device_id_type=MESH)
    for d in range(1, depth):
        pl.semaphore_signal(barrier, inc=1, device_id=(2 * lax.rem(z + d, depth) + y, ang), device_id_type=MESH)
    pl.semaphore_wait(barrier, depth)

    def y_copy(m):
        return pltpu.make_async_remote_copy(
            src_ref=part.at[m, 1 - y], dst_ref=y_recv.at[m],
            send_sem=ys_sem.at[m], recv_sem=yr_sem.at[m],
            device_id=(2 * z + 1 - y, ang), device_id_type=MESH)

    def z_copy(m, d):
        peer = lax.rem(z + d, depth)
        return pltpu.make_async_remote_copy(
            src_ref=part.at[m, y, peer], dst_ref=z_recv.at[m, d - 1],
            send_sem=zs_sem.at[m, d - 1], recv_sem=zr_sem.at[m, d - 1],
            device_id=(2 * peer + y, ang), device_id_type=MESH)

    def z_stage(m):
        y_copy(m).wait_recv()
        part[m, y] += y_recv[m]
        for d in range(depth - 1, 0, -1):
            z_copy(m, d).start()

    for m in range(chunks):
        def body(step, _):
            if m == 0:
                k_copy(step).wait()
            left, right = [], []
            for n in range(group):
                pair = step * group + n
                row = pl.multiple_of((first - 2 * pair + m * chunk) * slices, 16)
                left.append(w_ref[pl.ds(row, rows), :])
                right.append(jnp.concatenate([k_buf[2 * pair], k_buf[2 * pair + 1]], axis=1))
            product = jnp.dot(jnp.concatenate(left, axis=1), jnp.concatenate(right, axis=0),
                              preferred_element_type=jnp.float32)

            @pl.when(step == 0)
            def _():
                acc[...] = product

            @pl.when(step > 0)
            def _():
                acc[...] += product

            return 0

        lax.fori_loop(0, steps, body, 0)
        for b in range(slabs):
            tmp[b] = (acc[slices:slices + chunk * slices, 128 * b:128 * (b + 1)]
                      + acc[:chunk * slices, bins + 128 * b:bins + 128 * (b + 1)])
        for s in range(slices):
            for b in range(slabs):
                part[m, s % 2, s // 2, :, 128 * b:128 * (b + 1)] = tmp[b, pl.ds(s, chunk, stride=slices), :]
        y_copy(m).start()
        if m > 0:
            z_stage(m - 1)
    z_stage(chunks - 1)
    for m in range(chunks):
        total = part[m, y, z]
        for d in range(1, depth):
            z_copy(m, d).wait_recv()
            total += z_recv[m, d - 1]
        out_ref[0, m * chunk:(m + 1) * chunk, :] = total.astype(out_ref.dtype)
    for m in range(chunks):
        y_copy(m).wait_send()
        for d in range(1, depth):
            z_copy(m, d).wait_send()


def project(window, kernel_blocks, cuts, views, slices):
    offsets, radii, bins = kernel_blocks.shape
    group = split_of(offsets // 2, (3, 2))
    chunk = 48 if views % 48 == 0 else views
    chunks, depth = views // chunk, cuts // 2
    rows = (chunk + 2) * slices
    return pl.pallas_call(
        functools.partial(project_kernel, cuts, views, offsets, slices, group, chunk),
        out_shape=jax.ShapeDtypeStruct((1, views, bins), jnp.bfloat16),
        in_specs=[pl.BlockSpec(memory_space=pltpu.VMEM), pl.BlockSpec(memory_space=pl.ANY)],
        out_specs=pl.BlockSpec(memory_space=pltpu.VMEM),
        scratch_shapes=[
            pltpu.VMEM((offsets, radii, bins), jnp.bfloat16),
            pltpu.VMEM((rows, 2 * bins), jnp.float32),
            pltpu.VMEM((bins // 128, chunk * slices, 128), jnp.float32),
            pltpu.VMEM((chunks, 2, depth, chunk, bins), jnp.float32),
            pltpu.VMEM((chunks, depth, chunk, bins), jnp.float32),
            pltpu.VMEM((chunks, depth - 1, chunk, bins), jnp.float32),
            pltpu.SemaphoreType.DMA((offsets // (2 * group),)),
            pltpu.SemaphoreType.DMA((chunks,)),
            pltpu.SemaphoreType.DMA((chunks,)),
            pltpu.SemaphoreType.DMA((chunks, depth - 1)),
            pltpu.SemaphoreType.DMA((chunks, depth - 1)),
        ],
        compiler_params=pltpu.CompilerParams(
            collective_id=0, has_side_effects=True, vmem_limit_bytes=44 * 2**20),
        cost_estimate=pl.CostEstimate(
            flops=2 * views * slices * offsets * radii * bins,
            bytes_accessed=2 * offsets * radii * bins, transcendentals=0),
        name="project",
    )(window, kernel_blocks)


def gather_kernel(cuts, angles, views, offsets, d_ref, out_ref, turn, held,
                  as_sem, ar_sem, zs_sem, zr_sem, ys_sem, yr_sem):
    depth = cuts // 2
    cut = lax.axis_index("cuts")
    ang = lax.axis_index("angle")
    z, y = cut // 2, cut % 2

    def z_at(d):
        return lax.rem(z + d + depth, depth)

    def angle_at(d):
        return lax.rem(ang + d + angles, angles)

    def block_of(to_z, j):
        return lax.rem(ang - (2 * to_z * offsets) // views - 1 + j + 2 * angles, angles)

    barrier = pltpu.get_barrier_semaphore()
    pl.semaphore_signal(barrier, inc=1, device_id=(2 * z + 1 - y, ang), device_id_type=MESH)
    for d in range(1, depth):
        pl.semaphore_signal(barrier, inc=1, device_id=(2 * z_at(d) + y, ang), device_id_type=MESH)
    for d in range(1, angles):
        pl.semaphore_signal(barrier, inc=1, device_id=(cut, angle_at(d)), device_id_type=MESH)
    pl.semaphore_wait(barrier, depth + angles - 1)

    def angle_copy(d, slot):
        return pltpu.make_async_remote_copy(
            src_ref=d_ref.at[0], dst_ref=turn.at[slot],
            send_sem=as_sem.at[d - 1], recv_sem=ar_sem.at[d - 1],
            device_id=(cut, angle_at(d)), device_id_type=MESH)

    def z_copy(d, j, slot):
        return pltpu.make_async_remote_copy(
            src_ref=turn.at[block_of(z_at(d), j)], dst_ref=held.at[slot, j],
            send_sem=zs_sem.at[d - 1, j], recv_sem=zr_sem.at[d - 1, j],
            device_id=(2 * z_at(d) + y, ang), device_id_type=MESH)

    def y_copy(d, slot):
        return pltpu.make_async_remote_copy(
            src_ref=held.at[slot], dst_ref=held.at[slot],
            send_sem=ys_sem.at[d], recv_sem=yr_sem.at[d],
            device_id=(2 * z + 1 - y, ang), device_id_type=MESH)

    for d in range(1, angles):
        angle_copy(d, ang).start()
    turn[ang] = d_ref[0]
    for d in range(1, angles):
        angle_copy(d, angle_at(-d)).wait_recv()
    for d in range(1, depth):
        for j in range(2):
            z_copy(d, j, cut).start()
    for j in range(2):
        held[cut, j] = turn[block_of(z, j)]
    y_copy(0, cut).start()
    for d in range(1, depth):
        for j in range(2):
            z_copy(d, j, 2 * z_at(-d) + y).wait_recv()
        y_copy(d, 2 * z_at(-d) + y).start()
    for d in range(depth):
        y_copy(d, 2 * z_at(-d) + 1 - y).wait_recv()
    out_ref[...] = held[...]
    for d in range(1, angles):
        angle_copy(d, ang).wait_send()
    for d in range(1, depth):
        for j in range(2):
            z_copy(d, j, cut).wait_send()
    for d in range(depth):
        y_copy(d, 2 * z_at(-d) + y).wait_send()


def gather(density, offsets, cuts, angles):
    _, views, radii = density.shape
    depth = cuts // 2
    return pl.pallas_call(
        functools.partial(gather_kernel, cuts, angles, views, offsets),
        out_shape=jax.ShapeDtypeStruct((cuts, 2, views, radii), density.dtype),
        in_specs=[pl.BlockSpec(memory_space=pltpu.VMEM)],
        out_specs=pl.BlockSpec(memory_space=pltpu.VMEM),
        scratch_shapes=[
            pltpu.VMEM((angles, views, radii), density.dtype),
            pltpu.VMEM((cuts, 2, views, radii), density.dtype),
            pltpu.SemaphoreType.DMA((angles - 1,)),
            pltpu.SemaphoreType.DMA((angles - 1,)),
            pltpu.SemaphoreType.DMA((depth - 1, 2)),
            pltpu.SemaphoreType.DMA((depth - 1, 2)),
            pltpu.SemaphoreType.DMA((depth,)),
            pltpu.SemaphoreType.DMA((depth,)),
        ],
        compiler_params=pltpu.CompilerParams(
            collective_id=1, has_side_effects=True, vmem_limit_bytes=44 * 2**20),
        name="gather",
    )(density)


def local(density, kernel_blocks):
    _, views, radii = density.shape
    cuts = lax.axis_size("cuts")
    window = gather(density, kernel_blocks.shape[0], cuts, lax.axis_size("angle"))
    window = jnp.swapaxes(window.reshape(cuts, 2 * views, radii), 0, 1)
    rows = jnp.roll(window, -1, axis=0).reshape(2 * views * cuts, radii)
    return project(rows, kernel_blocks, cuts, views, cuts)


def solution(mesh):
    return jax.shard_map(
        local,
        mesh=mesh,
        in_specs=(P("cuts", "angle", None), P("cuts", None, None)),
        out_specs=P("cuts", "angle", None),
        check_vma=False,
    )
```

```python
import functools
import jax
import jax.numpy as jnp
from jax import lax
from jax.experimental import pallas as pl
from jax.experimental.pallas import tpu as pltpu
from jax.sharding import PartitionSpec as P

MESH = pl.DeviceIdType.MESH


def split_of(count, options):
    for n in options:
        if count % n == 0:
            return n
    return 1


def project_kernel(cuts, views, offsets, slices, group, sizes, w_ref, k_ref, out_ref,
                   k_buf, acc, tmp, part, y_recv, z_recv,
                   k_sem, ys_sem, yr_sem, zs_sem, zr_sem):
    bins = out_ref.shape[-1]
    slabs = bins // 128
    depth = cuts // 2
    steps = offsets // (2 * group)
    chunks = len(sizes)
    starts = [sum(sizes[:m]) for m in range(chunks)]
    cut = lax.axis_index("cuts")
    ang = lax.axis_index("angle")
    z, y = cut // 2, cut % 2
    first = views - (cut * offsets) % views - 2

    def k_copy(step):
        at = pl.ds(step * 2 * group, 2 * group)
        return pltpu.make_async_copy(k_ref.at[at], k_buf.at[at], k_sem.at[step])

    for step in range(steps):
        k_copy(step).start()

    barrier = pltpu.get_barrier_semaphore()
    pl.semaphore_signal(barrier, inc=1, device_id=(2 * z + 1 - y, ang), device_id_type=MESH)
    for d in range(1, depth):
        pl.semaphore_signal(barrier, inc=1, device_id=(2 * lax.rem(z + d, depth) + y, ang), device_id_type=MESH)
    pl.semaphore_wait(barrier, depth)

    def y_copy(m):
        return pltpu.make_async_remote_copy(
            src_ref=part.at[1 - y, :, pl.ds(starts[m], sizes[m])],
            dst_ref=y_recv.at[:, pl.ds(starts[m], sizes[m])],
            send_sem=ys_sem.at[m], recv_sem=yr_sem.at[m],
            device_id=(2 * z + 1 - y, ang), device_id_type=MESH)

    def z_copy(m, d):
        peer = lax.rem(z + d, depth)
        return pltpu.make_async_remote_copy(
            src_ref=part.at[y, peer, pl.ds(starts[m], sizes[m])],
            dst_ref=z_recv.at[d - 1, pl.ds(starts[m], sizes[m])],
            send_sem=zs_sem.at[m, d - 1], recv_sem=zr_sem.at[m, d - 1],
            device_id=(2 * peer + y, ang), device_id_type=MESH)

    def z_stage(m):
        y_copy(m).wait_recv()
        at = pl.ds(starts[m], sizes[m])
        part[y, :, at] += y_recv[:, at]
        for d in range(depth - 1, 0, -1):
            z_copy(m, d).start()

    for m in range(chunks):
        chunk, start = sizes[m], starts[m]
        rows = (chunk + 2) * slices

        def body(step, _):
            if m == 0:
                k_copy(step).wait()
            left, right = [], []
            for n in range(group):
                pair = step * group + n
                row = pl.multiple_of((first - 2 * pair + start) * slices, 16)
                left.append(w_ref[pl.ds(row, rows), :])
                right.append(jnp.concatenate([k_buf[2 * pair], k_buf[2 * pair + 1]], axis=1))
            product = jnp.dot(jnp.concatenate(left, axis=1), jnp.concatenate(right, axis=0),
                              preferred_element_type=jnp.float32)

            @pl.when(step == 0)
            def _():
                acc[:rows] = product

            @pl.when(step > 0)
            def _():
                acc[:rows] += product

            return 0

        lax.fori_loop(0, steps, body, 0)
        for b in range(slabs):
            tmp[b, :chunk * slices] = (acc[slices:slices + chunk * slices, 128 * b:128 * (b + 1)]
                      + acc[:chunk * slices, bins + 128 * b:bins + 128 * (b + 1)])
        for s in range(slices):
            for b in range(slabs):
                part[s % 2, s // 2, start:start + chunk, 128 * b:128 * (b + 1)] = tmp[b, pl.ds(s, chunk, stride=slices), :]
        y_copy(m).start()
        if m > 0:
            z_stage(m - 1)
    z_stage(chunks - 1)
    for m in range(chunks):
        at = pl.ds(starts[m], sizes[m])
        total = part[y, z, at]
        for d in range(1, depth):
            z_copy(m, d).wait_recv()
            total += z_recv[d - 1, at]
        out_ref[0, at, :] = total.astype(out_ref.dtype)
    for m in range(chunks):
        y_copy(m).wait_send()
        for d in range(1, depth):
            z_copy(m, d).wait_send()


def project(window, kernel_blocks, cuts, views, slices):
    offsets, radii, bins = kernel_blocks.shape
    group = split_of(offsets // 2, (3, 2))
    sizes = [48] * (views // 48 - 1) + [32, 16] if views % 48 == 0 else [views]
    chunk, chunks, depth = max(sizes), len(sizes), cuts // 2
    rows = (chunk + 2) * slices
    return pl.pallas_call(
        functools.partial(project_kernel, cuts, views, offsets, slices, group, sizes),
        out_shape=jax.ShapeDtypeStruct((1, views, bins), jnp.bfloat16),
        in_specs=[pl.BlockSpec(memory_space=pltpu.VMEM), pl.BlockSpec(memory_space=pl.ANY)],
        out_specs=pl.BlockSpec(memory_space=pltpu.VMEM),
        scratch_shapes=[
            pltpu.VMEM((offsets, radii, bins), jnp.bfloat16),
            pltpu.VMEM((rows, 2 * bins), jnp.float32),
            pltpu.VMEM((bins // 128, chunk * slices, 128), jnp.float32),
            pltpu.VMEM((2, depth, views, bins), jnp.float32),
            pltpu.VMEM((depth, views, bins), jnp.float32),
            pltpu.VMEM((depth - 1, views, bins), jnp.float32),
            pltpu.SemaphoreType.DMA((offsets // (2 * group),)),
            pltpu.SemaphoreType.DMA((chunks,)),
            pltpu.SemaphoreType.DMA((chunks,)),
            pltpu.SemaphoreType.DMA((chunks, depth - 1)),
            pltpu.SemaphoreType.DMA((chunks, depth - 1)),
        ],
        compiler_params=pltpu.CompilerParams(
            collective_id=0, has_side_effects=True, vmem_limit_bytes=44 * 2**20),
        cost_estimate=pl.CostEstimate(
            flops=2 * views * slices * offsets * radii * bins,
            bytes_accessed=2 * offsets * radii * bins, transcendentals=0),
        name="project",
    )(window, kernel_blocks)


def gather_kernel(cuts, angles, views, offsets, d_ref, out_ref, turn, held,
                  as_sem, ar_sem, zs_sem, zr_sem, ys_sem, yr_sem):
    depth = cuts // 2
    cut = lax.axis_index("cuts")
    ang = lax.axis_index("angle")
    z, y = cut // 2, cut % 2

    def z_at(d):
        return lax.rem(z + d + depth, depth)

    def angle_at(d):
        return lax.rem(ang + d + angles, angles)

    def block_of(to_z, j):
        return lax.rem(ang - (2 * to_z * offsets) // views - 1 + j + 2 * angles, angles)

    barrier = pltpu.get_barrier_semaphore()
    pl.semaphore_signal(barrier, inc=1, device_id=(2 * z + 1 - y, ang), device_id_type=MESH)
    for d in range(1, depth):
        pl.semaphore_signal(barrier, inc=1, device_id=(2 * z_at(d) + y, ang), device_id_type=MESH)
    for d in range(1, angles):
        pl.semaphore_signal(barrier, inc=1, device_id=(cut, angle_at(d)), device_id_type=MESH)
    pl.semaphore_wait(barrier, depth + angles - 1)

    def angle_copy(d, slot):
        return pltpu.make_async_remote_copy(
            src_ref=d_ref.at[0], dst_ref=turn.at[slot],
            send_sem=as_sem.at[d - 1], recv_sem=ar_sem.at[d - 1],
            device_id=(cut, angle_at(d)), device_id_type=MESH)

    def z_copy(d, j, slot):
        return pltpu.make_async_remote_copy(
            src_ref=turn.at[block_of(z_at(d), j)], dst_ref=held.at[slot, j],
            send_sem=zs_sem.at[d - 1, j], recv_sem=zr_sem.at[d - 1, j],
            device_id=(2 * z_at(d) + y, ang), device_id_type=MESH)

    def y_copy(d, slot):
        return pltpu.make_async_remote_copy(
            src_ref=held.at[slot], dst_ref=held.at[slot],
            send_sem=ys_sem.at[d], recv_sem=yr_sem.at[d],
            device_id=(2 * z + 1 - y, ang), device_id_type=MESH)

    for d in range(1, angles):
        angle_copy(d, ang).start()
    turn[ang] = d_ref[0]
    for d in range(1, angles):
        angle_copy(d, angle_at(-d)).wait_recv()
    for d in range(1, depth):
        for j in range(2):
            z_copy(d, j, cut).start()
    for j in range(2):
        held[cut, j] = turn[block_of(z, j)]
    y_copy(0, cut).start()
    for d in range(1, depth):
        for j in range(2):
            z_copy(d, j, 2 * z_at(-d) + y).wait_recv()
        y_copy(d, 2 * z_at(-d) + y).start()
    for d in range(depth):
        y_copy(d, 2 * z_at(-d) + 1 - y).wait_recv()
    out_ref[...] = held[...]
    for d in range(1, angles):
        angle_copy(d, ang).wait_send()
    for d in range(1, depth):
        for j in range(2):
            z_copy(d, j, cut).wait_send()
    for d in range(depth):
        y_copy(d, 2 * z_at(-d) + y).wait_send()


def gather(density, offsets, cuts, angles):
    _, views, radii = density.shape
    depth = cuts // 2
    return pl.pallas_call(
        functools.partial(gather_kernel, cuts, angles, views, offsets),
        out_shape=jax.ShapeDtypeStruct((cuts, 2, views, radii), density.dtype),
        in_specs=[pl.BlockSpec(memory_space=pltpu.VMEM)],
        out_specs=pl.BlockSpec(memory_space=pltpu.VMEM),
        scratch_shapes=[
            pltpu.VMEM((angles, views, radii), density.dtype),
            pltpu.VMEM((cuts, 2, views, radii), density.dtype),
            pltpu.SemaphoreType.DMA((angles - 1,)),
            pltpu.SemaphoreType.DMA((angles - 1,)),
            pltpu.SemaphoreType.DMA((depth - 1, 2)),
            pltpu.SemaphoreType.DMA((depth - 1, 2)),
            pltpu.SemaphoreType.DMA((depth,)),
            pltpu.SemaphoreType.DMA((depth,)),
        ],
        compiler_params=pltpu.CompilerParams(
            collective_id=1, has_side_effects=True, vmem_limit_bytes=44 * 2**20),
        name="gather",
    )(density)


def local(density, kernel_blocks):
    _, views, radii = density.shape
    cuts = lax.axis_size("cuts")
    window = gather(density, kernel_blocks.shape[0], cuts, lax.axis_size("angle"))
    window = jnp.swapaxes(window.reshape(cuts, 2 * views, radii), 0, 1)
    rows = jnp.roll(window, -1, axis=0).reshape(2 * views * cuts, radii)
    return project(rows, kernel_blocks, cuts, views, cuts)


def solution(mesh):
    return jax.shard_map(
        local,
        mesh=mesh,
        in_specs=(P("cuts", "angle", None), P("cuts", None, None)),
        out_specs=P("cuts", "angle", None),
        check_vma=False,
    )
```

```python
import functools
import jax
import jax.numpy as jnp
from jax import lax
from jax.experimental import pallas as pl
from jax.experimental.pallas import tpu as pltpu
from jax.sharding import PartitionSpec as P

MESH = pl.DeviceIdType.MESH


def split_of(count, options):
    for n in options:
        if count % n == 0:
            return n
    return 1


def project_kernel(cuts, views, offsets, slices, group, sizes, w_ref, k_ref, out_ref,
                   k_buf, acc, tmp, part, y_recv, z_recv,
                   k_sem, ys_sem, yr_sem, zs_sem, zr_sem):
    bins = out_ref.shape[-1]
    slabs = bins // 128
    depth = cuts // 2
    steps = offsets // (2 * group)
    chunks = len(sizes)
    starts = [sum(sizes[:m]) for m in range(chunks)]
    cut = lax.axis_index("cuts")
    ang = lax.axis_index("angle")
    z, y = cut // 2, cut % 2
    first = views - (cut * offsets) % views - 2

    def k_copy(step):
        at = pl.ds(step * 2 * group, 2 * group)
        return pltpu.make_async_copy(k_ref.at[at], k_buf.at[at], k_sem.at[step])

    for step in range(steps):
        k_copy(step).start()

    barrier = pltpu.get_barrier_semaphore()
    pl.semaphore_signal(barrier, inc=1, device_id=(2 * z + 1 - y, ang), device_id_type=MESH)
    for d in range(1, depth):
        pl.semaphore_signal(barrier, inc=1, device_id=(2 * lax.rem(z + d, depth) + y, ang), device_id_type=MESH)
    pl.semaphore_wait(barrier, depth)

    def y_copy(m):
        return pltpu.make_async_remote_copy(
            src_ref=part.at[1 - y, :, pl.ds(starts[m], sizes[m])],
            dst_ref=y_recv.at[:, pl.ds(starts[m], sizes[m])],
            send_sem=ys_sem.at[m], recv_sem=yr_sem.at[m],
            device_id=(2 * z + 1 - y, ang), device_id_type=MESH)

    def z_copy(m, d):
        peer = lax.rem(z + d, depth)
        return pltpu.make_async_remote_copy(
            src_ref=part.at[y, peer, pl.ds(starts[m], sizes[m])],
            dst_ref=z_recv.at[d - 1, pl.ds(starts[m], sizes[m])],
            send_sem=zs_sem.at[m, d - 1], recv_sem=zr_sem.at[m, d - 1],
            device_id=(2 * peer + y, ang), device_id_type=MESH)

    def z_stage(m):
        y_copy(m).wait_recv()
        at = pl.ds(starts[m], sizes[m])
        part[y, :, at] += y_recv[:, at]
        for d in range(depth - 1, 0, -1):
            z_copy(m, d).start()

    for m in range(chunks):
        chunk, start = sizes[m], starts[m]
        rows = (chunk + 2) * slices

        def body(step, _):
            if m == 0:
                k_copy(step).wait()
            left, right = [], []
            for n in range(group):
                pair = step * group + n
                row = pl.multiple_of((first - 2 * pair + start) * slices, 16)
                left.append(w_ref[pl.ds(row, rows), :])
                right.append(jnp.concatenate([k_buf[2 * pair], k_buf[2 * pair + 1]], axis=1))
            product = jnp.dot(jnp.concatenate(left, axis=1), jnp.concatenate(right, axis=0),
                              preferred_element_type=jnp.float32)

            @pl.when(step == 0)
            def _():
                acc[:rows] = product

            @pl.when(step > 0)
            def _():
                acc[:rows] += product

            return 0

        lax.fori_loop(0, steps, body, 0)
        for b in range(slabs):
            tmp[b, :chunk * slices] = (acc[slices:slices + chunk * slices, 128 * b:128 * (b + 1)]
                      + acc[:chunk * slices, bins + 128 * b:bins + 128 * (b + 1)])
        for s in range(slices):
            for b in range(slabs):
                part[s % 2, s // 2, start:start + chunk, 128 * b:128 * (b + 1)] = tmp[b, pl.ds(s, chunk, stride=slices), :]
        y_copy(m).start()
        if m > 0:
            z_stage(m - 1)
    z_stage(chunks - 1)
    for m in range(chunks):
        at = pl.ds(starts[m], sizes[m])
        total = part[y, z, at]
        for d in range(1, depth):
            z_copy(m, d).wait_recv()
            total += z_recv[d - 1, at]
        out_ref[0, at, :] = total.astype(out_ref.dtype)
    for m in range(chunks):
        y_copy(m).wait_send()
        for d in range(1, depth):
            z_copy(m, d).wait_send()


def project(window, kernel_blocks, cuts, views, slices):
    offsets, radii, bins = kernel_blocks.shape
    group = split_of(offsets // 2, (3, 2))
    sizes = [48] * (views // 48 - 1) + [32, 16] if views % 48 == 0 else [views]
    chunk, chunks, depth = max(sizes), len(sizes), cuts // 2
    rows = (chunk + 2) * slices
    return pl.pallas_call(
        functools.partial(project_kernel, cuts, views, offsets, slices, group, sizes),
        out_shape=jax.ShapeDtypeStruct((1, views, bins), jnp.bfloat16),
        in_specs=[pl.BlockSpec(memory_space=pltpu.VMEM), pl.BlockSpec(memory_space=pl.ANY)],
        out_specs=pl.BlockSpec(memory_space=pltpu.VMEM),
        scratch_shapes=[
            pltpu.VMEM((offsets, radii, bins), jnp.bfloat16),
            pltpu.VMEM((rows, 2 * bins), jnp.float32),
            pltpu.VMEM((bins // 128, chunk * slices, 128), jnp.float32),
            pltpu.VMEM((2, depth, views, bins), jnp.float32),
            pltpu.VMEM((depth, views, bins), jnp.float32),
            pltpu.VMEM((depth - 1, views, bins), jnp.float32),
            pltpu.SemaphoreType.DMA((offsets // (2 * group),)),
            pltpu.SemaphoreType.DMA((chunks,)),
            pltpu.SemaphoreType.DMA((chunks,)),
            pltpu.SemaphoreType.DMA((chunks, depth - 1)),
            pltpu.SemaphoreType.DMA((chunks, depth - 1)),
        ],
        compiler_params=pltpu.CompilerParams(
            collective_id=0, has_side_effects=True, vmem_limit_bytes=44 * 2**20),
        cost_estimate=pl.CostEstimate(
            flops=2 * views * slices * offsets * radii * bins,
            bytes_accessed=2 * offsets * radii * bins, transcendentals=0),
        name="project",
    )(window, kernel_blocks)


def gather_kernel(cuts, angles, views, offsets, d_ref, out_ref, turn, held,
                  as_sem, ar_sem, zs_sem, zr_sem, ys_sem, yr_sem):
    depth = cuts // 2
    cut = lax.axis_index("cuts")
    ang = lax.axis_index("angle")
    z, y = cut // 2, cut % 2

    def z_at(d):
        return lax.rem(z + d + depth, depth)

    def angle_at(d):
        return lax.rem(ang + d + angles, angles)

    def block_of(to_z, j):
        return lax.rem(ang - (2 * to_z * offsets) // views - 1 + j + 2 * angles, angles)

    barrier = pltpu.get_barrier_semaphore()
    pl.semaphore_signal(barrier, inc=1, device_id=(2 * z + 1 - y, ang), device_id_type=MESH)
    for d in range(1, depth):
        pl.semaphore_signal(barrier, inc=1, device_id=(2 * z_at(d) + y, ang), device_id_type=MESH)
    for d in range(1, angles):
        pl.semaphore_signal(barrier, inc=1, device_id=(cut, angle_at(d)), device_id_type=MESH)
    pl.semaphore_wait(barrier, depth + angles - 1)

    def angle_copy(d, slot):
        return pltpu.make_async_remote_copy(
            src_ref=d_ref.at[0], dst_ref=turn.at[slot],
            send_sem=as_sem.at[d - 1], recv_sem=ar_sem.at[d - 1],
            device_id=(cut, angle_at(d)), device_id_type=MESH)

    def z_copy(d, j, slot):
        return pltpu.make_async_remote_copy(
            src_ref=turn.at[block_of(z_at(d), j)], dst_ref=held.at[slot, j],
            send_sem=zs_sem.at[d - 1, j], recv_sem=zr_sem.at[d - 1, j],
            device_id=(2 * z_at(d) + y, ang), device_id_type=MESH)

    trim = min(offsets, views - offsets) // 16 * 16 if views % 16 == 0 else 0

    def y_copy(d, slot, to_y, short):
        if short:
            ref = held.at[slot, to_y, pl.ds(pl.multiple_of((1 - to_y) * trim, 16), views - trim)]
        else:
            ref = held.at[slot, 1 - to_y]
        return pltpu.make_async_remote_copy(
            src_ref=ref, dst_ref=ref,
            send_sem=ys_sem.at[d, short], recv_sem=yr_sem.at[d, short],
            device_id=(2 * z + 1 - y, ang), device_id_type=MESH)

    for d in range(1, angles):
        angle_copy(d, ang).start()
    turn[ang] = d_ref[0]
    for d in range(1, angles):
        angle_copy(d, angle_at(-d)).wait_recv()
    for d in range(1, depth):
        for j in range(2):
            z_copy(d, j, cut).start()
    for j in range(2):
        held[cut, j] = turn[block_of(z, j)]
    for short in range(2):
        y_copy(0, cut, 1 - y, short).start()
    for d in range(1, depth):
        for j in range(2):
            z_copy(d, j, 2 * z_at(-d) + y).wait_recv()
        for short in range(2):
            y_copy(d, 2 * z_at(-d) + y, 1 - y, short).start()
    for d in range(depth):
        slot = 2 * z_at(-d) + 1 - y
        if trim:
            rest = pl.ds(pl.multiple_of(y * (views - trim), 16), trim)
            held[slot, y, rest, :] = jnp.zeros((trim, held.shape[-1]), held.dtype)
        for short in range(2):
            y_copy(d, slot, y, short).wait_recv()
    out_ref[...] = held[...]
    for d in range(1, angles):
        angle_copy(d, ang).wait_send()
    for d in range(1, depth):
        for j in range(2):
            z_copy(d, j, cut).wait_send()
    for d in range(depth):
        for short in range(2):
            y_copy(d, 2 * z_at(-d) + y, 1 - y, short).wait_send()


def gather(density, offsets, cuts, angles):
    _, views, radii = density.shape
    depth = cuts // 2
    return pl.pallas_call(
        functools.partial(gather_kernel, cuts, angles, views, offsets),
        out_shape=jax.ShapeDtypeStruct((cuts, 2, views, radii), density.dtype),
        in_specs=[pl.BlockSpec(memory_space=pltpu.VMEM)],
        out_specs=pl.BlockSpec(memory_space=pltpu.VMEM),
        scratch_shapes=[
            pltpu.VMEM((angles, views, radii), density.dtype),
            pltpu.VMEM((cuts, 2, views, radii), density.dtype),
            pltpu.SemaphoreType.DMA((angles - 1,)),
            pltpu.SemaphoreType.DMA((angles - 1,)),
            pltpu.SemaphoreType.DMA((depth - 1, 2)),
            pltpu.SemaphoreType.DMA((depth - 1, 2)),
            pltpu.SemaphoreType.DMA((depth, 2)),
            pltpu.SemaphoreType.DMA((depth, 2)),
        ],
        compiler_params=pltpu.CompilerParams(
            collective_id=1, has_side_effects=True, vmem_limit_bytes=44 * 2**20),
        name="gather",
    )(density)


def local(density, kernel_blocks):
    _, views, radii = density.shape
    cuts = lax.axis_size("cuts")
    window = gather(density, kernel_blocks.shape[0], cuts, lax.axis_size("angle"))
    window = jnp.swapaxes(window.reshape(cuts, 2 * views, radii), 0, 1)
    rows = jnp.roll(window, -1, axis=0).reshape(2 * views * cuts, radii)
    return project(rows, kernel_blocks, cuts, views, cuts)


def solution(mesh):
    return jax.shard_map(
        local,
        mesh=mesh,
        in_specs=(P("cuts", "angle", None), P("cuts", None, None)),
        out_specs=P("cuts", "angle", None),
        check_vma=False,
    )
```
